32 devices in a mesh: dp: 16 (over z, x, core), seq: 2 (over y).
Axes of the slice: x: 2, y: 2, z: 4, core: 2. Of those that a mesh axis runs over, the one named last changes fastest.
Arguments:
- inputs: bfloat16 [32, 197, 768], P(('dp', 'seq')), may hold values from -6 to 6
- patch_order: int32 [32, 784], P(('dp', 'seq')), may hold values from 0 to 783, each once within a row
- image_count: int32 [16], P('dp'), may hold values from 0 to 1, as said below
- cotangent: bfloat16 [16, 784, 512], P('dp', 'seq'), may hold values from -6 to 6
- enc_gain_attn: float32 [768], replicated, may hold values from 0.1 to 1.9
- enc_shift_attn: float32 [768], replicated, may hold values from -3 to 3
- enc_project: bfloat16 [768, 2304], replicated, may hold values from -0.21875 to 0.21875
- enc_bias_query: float32 [768], replicated, may hold values from -3 to 3
- enc_bias_value: float32 [768], replicated, may hold values from -3 to 3
- enc_out: bfloat16 [768, 768], replicated, may hold values from -0.625 to 0.625
- enc_bias_out: float32 [768], replicated, may hold values from -3 to 3
- enc_gain_mlp: float32 [768], replicated, may hold values from 0.1 to 1.9
- enc_shift_mlp: float32 [768], replicated, may hold values from -3 to 3
- enc_up: bfloat16 [768, 3072], replicated, may hold values from -0.21875 to 0.21875
- enc_bias_up: float32 [3072], replicated, may hold values from -3 to 3
- enc_down: bfloat16 [3072, 768], replicated, may hold values from -0.109375 to 0.109375
- enc_bias_down: float32 [768], replicated, may hold values from -3 to 3
- embed_weight: bfloat16 [768, 512], replicated, may hold values from -0.21875 to 0.21875
- embed_bias: float32 [512], replicated, may hold values from -3 to 3
- mask_token: float32 [512], replicated, may hold values from -6 to 6
- dec_gain_attn: float32 [512], replicated, may hold values from 0.1 to 1.9
- dec_shift_attn: float32 [512], replicated, may hold values from -3 to 3
- dec_project: bfloat16 [512, 1536], replicated, may hold values from -0.25 to 0.25
- dec_bias_query: float32 [512], replicated, may hold values from -3 to 3
- dec_bias_value: float32 [512], replicated, may hold values from -3 to 3
- dec_out: bfloat16 [512, 512], replicated, may hold values from -1 to 1
- dec_bias_out: float32 [512], replicated, may hold values from -3 to 3
- dec_gain_mlp: float32 [512], replicated, may hold values from 0.1 to 1.9
- dec_shift_mlp: float32 [512], replicated, may hold values from -3 to 3
- dec_up: bfloat16 [512, 2048], replicated, may hold values from -0.25 to 0.25
- dec_bias_up: float32 [2048], replicated, may hold values from -3 to 3
- dec_down: bfloat16 [2048, 512], replicated, may hold values from -0.125 to 0.125
- dec_bias_down: float32 [512], replicated, may hold values from -3 to 3
Outputs:
- decoded: bfloat16 [16, 784, 512], P('dp', 'seq')
- input_grad: float32 [32, 197, 768], P(('dp', 'seq'))
- grad_enc_gain_attn: float32 [768], P('dp')
- grad_enc_shift_attn: float32 [768], P('dp')
- grad_enc_project: float32 [768, 2304], P('dp')
- grad_enc_bias_query: float32 [768], P('dp')
- grad_enc_bias_value: float32 [768], P('dp')
- grad_enc_out: float32 [768, 768], P('dp')
- grad_enc_bias_out: float32 [768], P('dp')
- grad_enc_gain_mlp: float32 [768], P('dp')
- grad_enc_shift_mlp: float32 [768], P('dp')
- grad_enc_up: float32 [768, 3072], P('dp')
- grad_enc_bias_up: float32 [3072], P('dp')
- grad_enc_down: float32 [3072, 768], P('dp')
- grad_enc_bias_down: float32 [768], P('dp')
- grad_embed_weight: float32 [768, 512], P('dp')
- grad_embed_bias: float32 [512], P('dp')
- grad_mask_token: float32 [512], P('dp')
- grad_dec_gain_attn: float32 [512], P('dp')
- grad_dec_shift_attn: float32 [512], P('dp')
- grad_dec_project: float32 [512, 1536], P('dp')
- grad_dec_bias_query: float32 [512], P('dp')
- grad_dec_bias_value: float32 [512], P('dp')
- grad_dec_out: float32 [512, 512], P('dp')
- grad_dec_bias_out: float32 [512], P('dp')
- grad_dec_gain_mlp: float32 [512], P('dp')
- grad_dec_shift_mlp: float32 [512], P('dp')
- grad_dec_up: float32 [512, 2048], P('dp')
- grad_dec_bias_up: float32 [2048], P('dp')
- grad_dec_down: float32 [2048, 512], P('dp')
- grad_dec_bias_down: float32 [512], P('dp')
The draws below stay inside these ranges and needn't reach their ends.
Inputs may be any that keep to these rules, and one draw needn't show every extreme that they name: Group g has image_count[g] live images: the first ones of its 1 image slots, in order; the other slots add nothing. `patch_order`: each row is a permutation of the 784 patches; its first 196 entries are the visible patches in encoder order, the rest are masked.
All inputs are finite; a program needn't handle non-finite values.
Results may differ from the reference program's by a relative error of at most 0.02.
Values may be sent and summed in bfloat16 or wider, within the bound.
A program may use at most 256 MiB of HBM per device.

```python
import jax
import jax.numpy as jnp
from jax import lax

D_ENC = 768
HEADS_ENC = 12
FF_ENC = 3072
D_DEC = 512
HEADS_DEC = 16
FF_DEC = 2048
GRID = 28
PATCHES = 784
VISIBLE = 196
ENC_LEN = 197
PPAD = 784
IMG_GRP = 1
IMAGES = 16
SLOTS = 32
N_DP = 16


def draw_image_count(key, part):
    key = jax.random.fold_in(key, 7)
    first, second, third = jax.random.split(key, 3)
    counts = jax.random.randint(first, (N_DP,), IMG_GRP // 2, IMG_GRP + 1)
    fullest = jax.random.randint(second, (), 0, N_DP)
    emptiest = (fullest + 1 + jax.random.randint(third, (), 0, N_DP - 1)) % N_DP
    counts = counts.at[fullest].set(IMG_GRP).at[emptiest].set(IMG_GRP // 2)
    return counts.astype(jnp.int32)


def block_scale(own_key, dims, cuts, least, largest):
    loudness, own = 1.0, jax.random.fold_in(own_key, 6)
    for axis_at, shards_of in cuts:
        draws = jnp.exp(jax.random.uniform(jax.random.fold_in(own, axis_at), (shards_of,), jnp.float32, least / len(cuts), largest / len(cuts)))
        loudness = loudness * jnp.repeat(draws, dims[axis_at] // shards_of).reshape([-1 if axis == axis_at else 1 for axis in range(len(dims))])
    return loudness


def bell_draw(key, extent, scale, most, cuts=(), held_as=jnp.bfloat16):
    array = jax.random.normal(key, extent, jnp.float32) * scale
    if len(cuts) > 0:
        array = block_scale(key, extent, cuts, -0.22, 0.18) * array
    return jnp.clip(array, min=-most, max=most).astype(held_as)


def setup_inputs(seed: int = 0) -> dict:
    arg_keys = jax.random.split(jax.random.key(seed), 34)
    return {
        "inputs": bell_draw(arg_keys[0], (SLOTS, ENC_LEN, D_ENC), 1.0, 6.0, ((0, 32),)),
        "patch_order": jax.vmap(lambda own: jax.random.permutation(own, PATCHES))(jax.random.split(arg_keys[1], SLOTS)).reshape((SLOTS, PATCHES)).astype(jnp.int32),
        "image_count": draw_image_count(jax.random.fold_in(arg_keys[33], 71), 0),
        "cotangent": bell_draw(arg_keys[3], (IMAGES, PPAD, D_DEC), 1.0, 6.0, ((0, 16), (1, 2))),
        "enc_gain_attn": jnp.clip(1.0 + 0.18 * jax.random.normal(arg_keys[4], (D_ENC,), jnp.float32), 0.1, 1.9),
        "enc_shift_attn": bell_draw(arg_keys[5], (D_ENC,), 0.5, 3.0, (), jnp.float32),
        "enc_project": bell_draw(arg_keys[6], (D_ENC, 3 * D_ENC), D_ENC ** -0.5, 0.21875),
        "enc_bias_query": bell_draw(arg_keys[7], (D_ENC,), 0.5, 3.0, (), jnp.float32),
        "enc_bias_value": bell_draw(arg_keys[8], (D_ENC,), 0.5, 3.0, (), jnp.float32),
        "enc_out": bell_draw(arg_keys[9], (D_ENC, D_ENC), (D_ENC // 8) ** -0.5, 0.625),
        "enc_bias_out": bell_draw(arg_keys[10], (D_ENC,), 0.5, 3.0, (), jnp.float32),
        "enc_gain_mlp": jnp.clip(1.0 + 0.18 * jax.random.normal(arg_keys[11], (D_ENC,), jnp.float32), 0.1, 1.9),
        "enc_shift_mlp": bell_draw(arg_keys[12], (D_ENC,), 0.5, 3.0, (), jnp.float32),
        "enc_up": bell_draw(arg_keys[13], (D_ENC, FF_ENC), D_ENC ** -0.5, 0.21875),
        "enc_bias_up": bell_draw(arg_keys[14], (FF_ENC,), 0.5, 3.0, (), jnp.float32),
        "enc_down": bell_draw(arg_keys[15], (FF_ENC, D_ENC), FF_ENC ** -0.5, 0.109375),
        "enc_bias_down": bell_draw(arg_keys[16], (D_ENC,), 0.5, 3.0, (), jnp.float32),
        "embed_weight": bell_draw(arg_keys[17], (D_ENC, D_DEC), D_ENC ** -0.5, 0.21875),
        "embed_bias": bell_draw(arg_keys[18], (D_DEC,), 0.5, 3.0, (), jnp.float32),
        "mask_token": bell_draw(arg_keys[19], (D_DEC,), 1.0, 6.0, (), jnp.float32),
        "dec_gain_attn": jnp.clip(1.0 + 0.18 * jax.random.normal(arg_keys[20], (D_DEC,), jnp.float32), 0.1, 1.9),
        "dec_shift_attn": bell_draw(arg_keys[21], (D_DEC,), 0.5, 3.0, (), jnp.float32),
        "dec_project": bell_draw(arg_keys[22], (D_DEC, 3 * D_DEC), D_DEC ** -0.5, 0.25),
        "dec_bias_query": bell_draw(arg_keys[23], (D_DEC,), 0.5, 3.0, (), jnp.float32),
        "dec_bias_value": bell_draw(arg_keys[24], (D_DEC,), 0.5, 3.0, (), jnp.float32),
        "dec_out": bell_draw(arg_keys[25], (D_DEC, D_DEC), (D_DEC // 16) ** -0.5, 1.0),
        "dec_bias_out": bell_draw(arg_keys[26], (D_DEC,), 0.5, 3.0, (), jnp.float32),
        "dec_gain_mlp": jnp.clip(1.0 + 0.18 * jax.random.normal(arg_keys[27], (D_DEC,), jnp.float32), 0.1, 1.9),
        "dec_shift_mlp": bell_draw(arg_keys[28], (D_DEC,), 0.5, 3.0, (), jnp.float32),
        "dec_up": bell_draw(arg_keys[29], (D_DEC, FF_DEC), D_DEC ** -0.5, 0.25),
        "dec_bias_up": bell_draw(arg_keys[30], (FF_DEC,), 0.5, 3.0, (), jnp.float32),
        "dec_down": bell_draw(arg_keys[31], (FF_DEC, D_DEC), FF_DEC ** -0.5, 0.125),
        "dec_bias_down": bell_draw(arg_keys[32], (D_DEC,), 0.5, 3.0, (), jnp.float32),
    }


@jax.custom_vjp
def low(v):
    return lax.optimization_barrier(v.astype(jnp.bfloat16)).astype(jnp.float32)

@jax.custom_vjp
def low_back(v):
    return v

def low_keep(v):
    return (low(v), None)

def low_pass(kept, grad):
    return (grad,)

def back_keep(v):
    return (v, None)

def back_low(kept, grad):
    return (low(grad),)
low.defvjp(low_keep, low_pass)
low_back.defvjp(back_keep, back_low)

def matmul(left, right):
    return jnp.dot(left, right, precision=lax.Precision.HIGHEST, preferred_element_type=jnp.float32)

def normalize(rows, gain, shift):
    center = rows - lax.optimization_barrier(jnp.mean(rows, axis=-1, keepdims=True))
    spread = lax.optimization_barrier(jnp.mean(center * center, axis=-1, keepdims=True))
    return center * lax.rsqrt(spread + 1e-06) * gain + shift

def positions(grid, width):
    quarter = width // 4
    omega = 1.0 / 10000.0 ** (jnp.arange(quarter).astype(jnp.float32) / quarter)
    place = jnp.arange(grid * grid)
    first = (place // grid).astype(jnp.float32)[:, None] * omega[None, :]
    second = (place % grid).astype(jnp.float32)[:, None] * omega[None, :]
    return jnp.concatenate([jnp.sin(first), jnp.cos(first), jnp.sin(second), jnp.cos(second)], axis=1)

def attend(query, keys, values, heads):
    images, length, width = query.shape
    size = width // heads
    shape = (images, length, heads, size)
    scores = jnp.einsum('bqhd,bkhd->bhqk', query.reshape(shape), keys.reshape(shape), precision=lax.Precision.HIGHEST) * size ** (-0.5)
    top = lax.optimization_barrier(jnp.max(scores, axis=-1, keepdims=True))
    weights = jnp.exp(scores - top)
    weights = weights / lax.optimization_barrier(jnp.sum(weights, axis=-1, keepdims=True))
    mixed = jnp.einsum('bhqk,bkhd->bqhd', weights, values.reshape(shape), precision=lax.Precision.HIGHEST)
    return mixed.reshape(images, length, width)

def block(rows, params, heads):
    gain_a, shift_a, w_project, bias_query, bias_value, w_out, bias_out, gain_b, shift_b, w_up, bias_up, w_down, bias_down = params
    width = rows.shape[-1]
    normed = low(normalize(rows, gain_a, shift_a))
    project = matmul(normed, w_project)
    query = low(low_back(project[..., :width] + bias_query))
    keys = low(low_back(project[..., width:2 * width]))
    values = low(low_back(project[..., 2 * width:] + bias_value))
    mixed = low(attend(query, keys, values, heads))
    branch = low_back(matmul(mixed, w_out) + bias_out)
    middle = rows + branch
    inner = low_back(matmul(low(normalize(middle, gain_b, shift_b)), w_up) + bias_up)
    active = low(jax.nn.gelu(inner, approximate=False))
    return middle + low_back(matmul(active, w_down) + bias_down)

def forward(weights, rows, order, live):
    encoder, embed_weight, embed_bias, mask_token, decoder = weights
    encoded = block(rows, encoder, HEADS_ENC)
    visible = matmul(low(encoded[:, 1:, :]), embed_weight) + embed_bias
    count = rows.shape[0]
    tokens = jnp.broadcast_to(mask_token, (count, PATCHES, D_DEC))
    tokens = tokens.at[jnp.arange(count)[:, None], order[:, :VISIBLE]].set(visible)
    tokens = low(low_back(tokens + positions(GRID, D_DEC)))
    decoded = block(tokens, decoder, HEADS_DEC)
    decoded = jnp.pad(decoded, ((0, 0), (0, PPAD - PATCHES), (0, 0)))
    return decoded * live[:, None, None]

def reference(inputs, patch_order, image_count, cotangent, enc_gain_attn, enc_shift_attn, enc_project, enc_bias_query, enc_bias_value, enc_out, enc_bias_out, enc_gain_mlp, enc_shift_mlp, enc_up, enc_bias_up, enc_down, enc_bias_down, embed_weight, embed_bias, mask_token, dec_gain_attn, dec_shift_attn, dec_project, dec_bias_query, dec_bias_value, dec_out, dec_bias_out, dec_gain_mlp, dec_shift_mlp, dec_up, dec_bias_up, dec_down, dec_bias_down):
    encoder = tuple((item.astype(jnp.float32) for item in (enc_gain_attn, enc_shift_attn, enc_project, enc_bias_query, enc_bias_value, enc_out, enc_bias_out, enc_gain_mlp, enc_shift_mlp, enc_up, enc_bias_up, enc_down, enc_bias_down)))
    decoder = tuple((item.astype(jnp.float32) for item in (dec_gain_attn, dec_shift_attn, dec_project, dec_bias_query, dec_bias_value, dec_out, dec_bias_out, dec_gain_mlp, dec_shift_mlp, dec_up, dec_bias_up, dec_down, dec_bias_down)))
    weights = (encoder, embed_weight.astype(jnp.float32), embed_bias.astype(jnp.float32), mask_token.astype(jnp.float32), decoder)
    alive = (jnp.arange(IMAGES) % IMG_GRP < jnp.repeat(image_count, IMG_GRP)).astype(jnp.float32)
    groups = N_DP
    slot_rows = inputs.astype(jnp.float32).reshape(groups, 2 * IMG_GRP, ENC_LEN, D_ENC)[:, 0::2]
    slot_order = patch_order.reshape(groups, 2 * IMG_GRP, PATCHES)[:, 0::2]
    pieces = (slot_rows.reshape(IMAGES, 1, ENC_LEN, D_ENC), slot_order.reshape(IMAGES, 1, PATCHES), alive.reshape(IMAGES, 1), cotangent.astype(jnp.float32).reshape(IMAGES, 1, PPAD, D_DEC))
    zeros = jax.tree.map(jnp.zeros_like, weights)

    def visit(totals, piece):
        rows, order, live, start_grad = piece

        def run(params, rows_in):
            return forward(params, rows_in, order, live)
        output, pull = jax.vjp(run, weights, rows)
        grad_params, grad_rows = pull(start_grad)
        return (jax.tree.map(jnp.add, totals, grad_params), (output.astype(jnp.bfloat16), grad_rows))
    totals, outputs = lax.scan(visit, zeros, pieces)
    decoded = outputs[0].reshape(IMAGES, PPAD, D_DEC)
    image_grads = outputs[1].reshape(groups, IMG_GRP, ENC_LEN, D_ENC)
    input_grad = jnp.zeros((groups, 2 * IMG_GRP, ENC_LEN, D_ENC), jnp.float32).at[:, 0::2].set(image_grads)
    input_grad = input_grad.reshape(SLOTS, ENC_LEN, D_ENC)
    enc_grads = totals[0]
    dec_grads = totals[4]
    return (decoded, input_grad, enc_grads[0], enc_grads[1], enc_grads[2], enc_grads[3], enc_grads[4], enc_grads[5], enc_grads[6], enc_grads[7], enc_grads[8], enc_grads[9], enc_grads[10], enc_grads[11], enc_grads[12], totals[1], totals[2], totals[3], dec_grads[0], dec_grads[1], dec_grads[2], dec_grads[3], dec_grads[4], dec_grads[5], dec_grads[6], dec_grads[7], dec_grads[8], dec_grads[9], dec_grads[10], dec_grads[11], dec_grads[12])
```

```python
from functools import partial

import jax
import jax.numpy as jnp
import numpy as np
from jax import lax
from jax.experimental import pallas as pl
from jax.experimental.pallas import tpu as pltpu
from jax.sharding import PartitionSpec as P

HEADS_ENC = 12
HEADS_DEC = 16
GRID = 28
PATCHES = 784
VISIBLE = 196


exact_mode = lax.Precision.HIGHEST


def from_behind(x, axis, by):
    devices = lax.axis_size(axis)
    return lax.ppermute(x, axis, [(i, (i + by) % devices) for i in range(devices)])


def normalize(rows, gain, shift):
    center = rows - jnp.mean(rows, axis=-1, keepdims=True)
    spread = jnp.mean(center * center, axis=-1, keepdims=True)
    return center * lax.rsqrt(spread + 1e-06) * gain + shift


def positions(grid, width):
    quarter = width // 4
    omega = 1.0 / 10000.0 ** (jnp.arange(quarter).astype(jnp.float32) / quarter)
    place = jnp.arange(grid * grid)
    first = (place // grid).astype(jnp.float32)[:, None] * omega[None, :]
    second = (place % grid).astype(jnp.float32)[:, None] * omega[None, :]
    return jnp.concatenate(
        [jnp.sin(first), jnp.cos(first), jnp.sin(second), jnp.cos(second)], axis=1
    )


def gelu_exact(inner):
    return jax.nn.gelu(inner, approximate=False)


def product(left, right):
    return jnp.dot(left, right, preferred_element_type=jnp.float32)


def transposed(grad, weight):
    return jnp.einsum("...j,ij->...i", grad, weight, preferred_element_type=jnp.float32)


def outer(left, grad):
    return jnp.einsum("...i,...j->ij", left, grad, preferred_element_type=jnp.float32)


def column_sum(grad):
    return jnp.sum(grad.astype(jnp.float32), axis=(0, 1))


def attend(query, keys, values, heads, key_valid):
    images, length, width = query.shape
    size = width // heads
    query = query.reshape(images, length, heads, size)
    keys = keys.reshape(images, keys.shape[1], heads, size)
    values = values.reshape(images, values.shape[1], heads, size)
    scores = jnp.einsum("bqhd,bkhd->bhqk", query, keys, precision=exact_mode) * size ** (-0.5)
    top = jnp.max(scores, axis=-1, keepdims=True)
    weights = jnp.exp(scores - top)
    weights = weights / jnp.sum(weights, axis=-1, keepdims=True)
    mixed = jnp.einsum("bhqk,bkhd->bqhd", weights, values, precision=exact_mode)
    return mixed.reshape(images, length, width)


def local_attend(query, keys, values):
    mixed = attend(
        query.astype(jnp.float32),
        keys.astype(jnp.float32),
        values.astype(jnp.float32),
        HEADS_ENC,
        None,
    )
    return (mixed, None)


def local_attend_back(grad_mixed, query, keys, values, saved):
    local = partial(attend, heads=HEADS_ENC, key_valid=None)
    pull = jax.vjp(
        local, query.astype(jnp.float32), keys.astype(jnp.float32), values.astype(jnp.float32)
    )[1]
    return pull(grad_mixed)


def block_forward(rows, params, attend_fn):
    (
        gain_a,
        shift_a,
        w_project,
        bias_query,
        bias_value,
        w_out,
        bias_out,
        gain_b,
        shift_b,
        w_up,
        bias_up,
        w_down,
        bias_down,
    ) = params
    width = rows.shape[-1]
    normed = normalize(rows, gain_a, shift_a).astype(jnp.bfloat16)
    project = product(normed, w_project)
    query = (project[..., :width] + bias_query).astype(jnp.bfloat16)
    keys = project[..., width : 2 * width].astype(jnp.bfloat16)
    values = (project[..., 2 * width :] + bias_value).astype(jnp.bfloat16)
    mixed, saved = attend_fn(query, keys, values)
    mixed_low = mixed.astype(jnp.bfloat16)
    middle = rows + (product(mixed_low, w_out) + bias_out)
    normed_b = normalize(middle, gain_b, shift_b).astype(jnp.bfloat16)
    inner = product(normed_b, w_up) + bias_up
    active = gelu_exact(inner).astype(jnp.bfloat16)
    result = middle + (product(active, w_down) + bias_down)
    return (
        result,
        (rows, normed, query, keys, values, saved, mixed_low, middle, normed_b, inner, active),
    )


def block_backward(grad, params, cache, attend_back):
    (
        gain_a,
        shift_a,
        w_project,
        bias_query,
        bias_value,
        w_out,
        bias_out,
        gain_b,
        shift_b,
        w_up,
        bias_up,
        w_down,
        bias_down,
    ) = params
    rows, normed, query, keys, values, saved, mixed_low, middle, normed_b, inner, active = cache
    width = rows.shape[-1]
    grad_down = grad.astype(jnp.bfloat16)
    grad_w_down = outer(active, grad_down)
    grad_b_down = column_sum(grad_down)
    grad_active = transposed(grad_down, w_down)
    grad_inner = jax.vjp(gelu_exact, inner)[1](grad_active)[0].astype(jnp.bfloat16)
    grad_w_up = outer(normed_b, grad_inner)
    grad_b_up = column_sum(grad_inner)
    grad_normed_b = transposed(grad_inner, w_up)
    grad_mid_part, grad_gain_b, grad_shift_b = jax.vjp(normalize, middle, gain_b, shift_b)[1](
        grad_normed_b
    )
    grad_middle = grad + grad_mid_part
    grad_out = grad_middle.astype(jnp.bfloat16)
    grad_w_out = outer(mixed_low, grad_out)
    grad_b_out = column_sum(grad_out)
    grad_mixed = transposed(grad_out, w_out)
    grad_query, grad_keys, grad_values = attend_back(grad_mixed, query, keys, values, saved)
    grad_project = jnp.concatenate(
        [
            grad_query.astype(jnp.bfloat16),
            grad_keys.astype(jnp.bfloat16),
            grad_values.astype(jnp.bfloat16),
        ],
        axis=-1,
    )
    grad_w_project = outer(normed, grad_project)
    grad_b_query = column_sum(grad_project[..., :width])
    grad_b_value = column_sum(grad_project[..., 2 * width :])
    grad_normed = transposed(grad_project, w_project)
    grad_rows_part, grad_gain_a, grad_shift_a = jax.vjp(normalize, rows, gain_a, shift_a)[1](
        grad_normed
    )
    grads = (
        grad_gain_a,
        grad_shift_a,
        grad_w_project,
        grad_b_query,
        grad_b_value,
        grad_w_out,
        grad_b_out,
        grad_gain_b,
        grad_shift_b,
        grad_w_up,
        grad_b_up,
        grad_w_down,
        grad_b_down,
    )
    return (grad_middle + grad_rows_part, grads)


def pack(grads, parts):
    return jnp.concatenate([grad.reshape(parts, -1) for grad in grads], axis=1)


def unpack(flat, grads, parts):
    pieces = []
    start = 0
    for grad in grads:
        width = grad.size // parts
        pieces.append(
            flat[:, start : start + width].reshape((grad.shape[0] // parts,) + grad.shape[1:])
        )
        start = start + width
    return pieces


def reduce_whole(grads, parts):
    shares = lax.psum_scatter(
        pack(grads, parts).astype(jnp.bfloat16), "dp", scatter_dimension=0, tiled=True
    )
    return unpack(lax.psum(shares, "seq").astype(jnp.float32), grads, parts)


def per_device(
    inputs,
    patch_order,
    image_count,
    cotangent,
    enc_gain_attn,
    enc_shift_attn,
    enc_project,
    enc_bias_query,
    enc_bias_value,
    enc_out,
    enc_bias_out,
    enc_gain_mlp,
    enc_shift_mlp,
    enc_up,
    enc_bias_up,
    enc_down,
    enc_bias_down,
    embed_weight,
    embed_bias,
    mask_token,
    dec_gain_attn,
    dec_shift_attn,
    dec_project,
    dec_bias_query,
    dec_bias_value,
    dec_out,
    dec_bias_out,
    dec_gain_mlp,
    dec_shift_mlp,
    dec_up,
    dec_bias_up,
    dec_down,
    dec_bias_down,
):
    seq_size = lax.axis_size("seq")
    seq_rank = lax.axis_index("seq")
    data_size = lax.axis_size("dp")
    local_images = inputs.shape[0]
    group_images, block_rows, dec_width = cotangent.shape
    head_size = dec_width // HEADS_DEC
    scale = head_size ** (-0.5)
    encoder = (
        enc_gain_attn,
        enc_shift_attn,
        enc_project,
        enc_bias_query,
        enc_bias_value,
        enc_out,
        enc_bias_out,
        enc_gain_mlp,
        enc_shift_mlp,
        enc_up,
        enc_bias_up,
        enc_down,
        enc_bias_down,
    )
    decoder = (
        dec_gain_attn,
        dec_shift_attn,
        dec_project,
        dec_bias_query,
        dec_bias_value,
        dec_out,
        dec_bias_out,
        dec_gain_mlp,
        dec_shift_mlp,
        dec_up,
        dec_bias_up,
        dec_down,
        dec_bias_down,
    )
    live_count = image_count[0]
    group_alive = (jnp.arange(group_images) < live_count).astype(jnp.float32)
    own_patches = seq_rank * block_rows + jnp.arange(block_rows)
    row_keep = (own_patches < PATCHES).astype(jnp.float32)
    keep = group_alive[:, None, None] * row_keep[None, :, None]
    shape4 = (group_images, block_rows, HEADS_DEC, head_size)

    def valid_from(turn):
        source = (seq_rank - turn) % seq_size
        return (source * block_rows + jnp.arange(block_rows) < PATCHES)[None, None, None, :]

    def cycle_attend(query, keys, values):
        query4 = query.reshape(shape4)
        top = None
        for turn in range(seq_size):
            if turn > 0:
                keys, values = from_behind((keys, values), "seq", 1)
            keys4 = keys.reshape(shape4)
            values4 = values.reshape(shape4).astype(jnp.float32)
            scores = (
                jnp.einsum("iqhd,ikhd->ihqk", query4, keys4, preferred_element_type=jnp.float32)
                * scale
            )
            scores = jnp.where(valid_from(turn), scores, -jnp.inf)
            block_top = jnp.max(scores, axis=-1, keepdims=True)
            if top is None:
                top = block_top
                weights = jnp.exp(scores - top)
                total = jnp.sum(weights, axis=-1, keepdims=True)
                gathered = jnp.einsum("ihqk,ikhd->ihqd", weights, values4, precision=exact_mode)
            else:
                new_top = jnp.maximum(top, block_top)
                fade = jnp.exp(top - new_top)
                weights = jnp.exp(scores - new_top)
                total = total * fade + jnp.sum(weights, axis=-1, keepdims=True)
                gathered = gathered * fade + jnp.einsum(
                    "ihqk,ikhd->ihqd", weights, values4, precision=exact_mode
                )
                top = new_top
        mixed = (
            (gathered / total).transpose(0, 2, 1, 3).reshape(group_images, block_rows, dec_width)
        )
        return (mixed, (mixed, top + jnp.log(total)))

    def cycle_back(grad_mixed, query, keys, values, saved):
        mixed, log_total = saved
        grad4 = grad_mixed.reshape(shape4)
        query4 = query.reshape(shape4)
        query_wide = query4.astype(jnp.float32)
        delta = jnp.sum(grad4 * mixed.reshape(shape4), axis=-1).transpose(0, 2, 1)[..., None]
        grad_query = jnp.zeros(shape4, jnp.float32)
        grad_keys = jnp.zeros(shape4, jnp.float32)
        grad_values = jnp.zeros(shape4, jnp.float32)
        for turn in range(seq_size):
            if turn > 0:
                keys, values = from_behind((keys, values), "seq", 1)
            keys4 = keys.reshape(shape4)
            keys_wide = keys4.astype(jnp.float32)
            values_wide = values.reshape(shape4).astype(jnp.float32)
            scores = (
                jnp.einsum("iqhd,ikhd->ihqk", query4, keys4, preferred_element_type=jnp.float32)
                * scale
            )
            scores = jnp.where(valid_from(turn), scores, -jnp.inf)
            weights = jnp.exp(scores - log_total)
            grad_values = grad_values + jnp.einsum(
                "ihqk,iqhd->ikhd", weights, grad4, precision=exact_mode
            )
            grad_weights = jnp.einsum("iqhd,ikhd->ihqk", grad4, values_wide, precision=exact_mode)
            grad_scores = weights * (grad_weights - delta) * scale
            grad_query = grad_query + jnp.einsum(
                "ihqk,ikhd->iqhd", grad_scores, keys_wide, precision=exact_mode
            )
            grad_keys = grad_keys + jnp.einsum(
                "ihqk,iqhd->ikhd", grad_scores, query_wide, precision=exact_mode
            )
            grad_keys, grad_values = (
                from_behind(grad_keys.astype(jnp.bfloat16), "seq", 1).astype(grad_keys.dtype),
                from_behind(grad_values.astype(jnp.bfloat16), "seq", 1).astype(grad_values.dtype),
            )
        flat_shape = (group_images, block_rows, dec_width)
        return (
            grad_query.reshape(flat_shape),
            grad_keys.reshape(flat_shape),
            grad_values.reshape(flat_shape),
        )

    rows = inputs.astype(jnp.float32)
    encoded, enc_cache = block_forward(rows, encoder, local_attend)
    seen = encoded[:, 1:, :].astype(jnp.bfloat16)
    visible = product(seen, embed_weight) + embed_bias
    image_ids = jnp.arange(local_images)[:, None]
    slots = patch_order[:, :VISIBLE]
    tokens = jnp.broadcast_to(mask_token, (local_images, PATCHES, dec_width))
    tokens = tokens.at[image_ids, slots].set(visible)
    tokens = tokens + positions(GRID, dec_width)
    tokens = tokens.astype(jnp.bfloat16)
    arrived = lax.all_to_all(tokens, "seq", split_axis=1, concat_axis=0, tiled=True)
    block_tokens = arrived[0::2]
    decoded, dec_cache = block_forward(block_tokens.astype(jnp.float32), decoder, cycle_attend)
    result = (decoded * keep).astype(jnp.bfloat16)
    start_grad = cotangent.astype(jnp.float32) * keep
    grad_tokens, dec_grads = block_backward(start_grad, decoder, dec_cache, cycle_back)
    spread_back = (
        jnp.zeros((seq_size, block_rows, dec_width), jnp.bfloat16)
        .at[0::2]
        .set(grad_tokens.astype(jnp.bfloat16))
    )
    returned = lax.all_to_all(spread_back, "seq", split_axis=0, concat_axis=1, tiled=True)
    grad_visible = returned[image_ids, slots]
    shown = jnp.zeros((local_images, PATCHES), jnp.float32).at[image_ids, slots].set(1.0)
    grad_mask = jnp.sum(returned.astype(jnp.float32) * (1.0 - shown)[:, :, None], axis=(0, 1))
    grad_embed_weight = outer(seen, grad_visible)
    grad_embed_bias = column_sum(grad_visible)
    grad_seen = transposed(grad_visible, embed_weight)
    grad_encoded = jnp.pad(grad_seen, ((0, 0), (1, 0), (0, 0)))
    again = lax.optimization_barrier(rows)
    enc_cache = block_forward(again, encoder, local_attend)[1]
    grad_rows, enc_grads = block_backward(grad_encoded, encoder, enc_cache, local_attend_back)
    tail = list(enc_grads) + [grad_embed_weight, grad_embed_bias, grad_mask]
    summed = reduce_whole(tail + list(dec_grads), data_size)
    return (result, grad_rows) + tuple(summed)


BF = jnp.bfloat16
F32 = jnp.float32
MESH = pl.DeviceIdType.MESH
WHOLE = pl.BlockSpec(memory_space=pltpu.VMEM)
ANYWHERE = pl.BlockSpec(memory_space=pl.ANY)
ROWS = 208
LANES = 128
VMEM_CAP = 63 * 1024 * 1024
PAIRS = HEADS_ENC // 2
STEP_HEADS = 2
D_DOWN, D_UP, D_OUT, D_PROJECT = 0, 256, 512, 576
E_EMBED, E_DOWN, E_UP, E_OUT, E_PROJECT, E_VECTOR = 768, 864, 1440, 2016, 2160, 2592
V_ROWS = 32
D_ROWS = 768
T_ROWS = E_VECTOR + V_ROWS
CHUNKS = (
    (0, 256), (256, 320), (576, 192), (768, 96), (864, 384), (1248, 192), (1440, 192), (1632,
    192), (1824, 192), (2016, 144), (2160, 224), (2384, 160), (2544, 80),
)
X_DONE = (4, 5)
Z_FIRST = ()
PLAN = {
    "heads": ((0, "c"),),
    "heads0": ((1, "c"),),
    "heads1": ((0, "x"),),
    "heads2": ((0, "z0"),),
    "after_heads": ((0, "z1"), (1, "x"),),
    "gathered": ((0, "z2"), (1, "z0"),),
    "embed": ((2, "c"),),
    "part2": ((3, "c"),),
    "up2": ((2, "x"),),
    "down": ((6, "c"),),
    "norm": ((7, "c"), (2, "z0"), (8, "c"),),
    "out": ((4, "c"), (5, "c"), (3, "x"),),
    "sums": ((2, "z1"),),
    "pair1": ((9, "c"), (4, "z0"), (6, "x"),),
    "pair2": ((5, "z0"), (3, "z0"),),
    "pair3": ((2, "z2"),),
    "pair5": ((7, "x"), (4, "z1"),),
    "project": ((6, "z0"), (5, "z1"),),
    "vectors": ((3, "z1"), (7, "z0"), (8, "x"), (10, "c"),),
    "after": (
        (11, "c"), (4, "z2"), (6, "z1"), (9, "x"), (12, "c"), (5, "z2"), (3, "z2"), (7,
        "z1"), (8, "z0"), (6, "z2"), (10, "x"), (9, "z0"), (7, "z2"), (8, "z1"), (11, "x"),
        (10, "z0"), (9, "z1"), (12, "x"), (8, "z2"), (11, "z0"), (10, "z1"), (9, "z2"), (12,
        "z0"), (11, "z1"), (10, "z2"), (12, "z1"), (11, "z2"), (12, "z2"),
    ),
    "open": ((1, "z1"),),
    "part0": ((1, "z2"),),
}


def mul(left, right, left_dim=1, right_dim=0):
    return lax.dot_general(
        left, right, (((left_dim,), (right_dim,)), ((), ())), preferred_element_type=F32
    )


def row_of(ref):
    return ref[...][None, :]


def standard(rows):
    center = rows - jnp.mean(rows, axis=-1, keepdims=True)
    scale = lax.rsqrt(jnp.mean(center * center, axis=-1, keepdims=True) + 1e-06)
    return center * scale, scale


def standard_back(unit, scale, grad):
    return scale * (
        grad
        - jnp.mean(grad, axis=-1, keepdims=True)
        - unit * jnp.mean(grad * unit, axis=-1, keepdims=True)
    )


def gelu_pair(inner):
    half = 0.5 + 0.5 * lax.erf(inner * 0.7071067811865476)
    bell = jnp.exp(inner * inner * -0.5) * 0.3989422804014327
    return inner * half, half + inner * bell


def sums(rows):
    return jnp.sum(rows, axis=0, keepdims=True)


def shares_of(row, total, first=0):
    n = row.shape[1]
    width = total // 16
    lanes = -(-width // LANES) * LANES
    at = lax.broadcasted_iota(jnp.int32, (16, n), 1) + first
    start = lax.broadcasted_iota(jnp.int32, (16, n), 0) * width
    inside = (at >= start) & (at < start + width)
    own = jnp.where(inside, jnp.broadcast_to(row, (16, n)), 0.0).astype(BF)
    eye = lax.broadcasted_iota(jnp.int32, (width, lanes), 0) == lax.broadcasted_iota(
        jnp.int32, (width, lanes), 1
    )
    place = jnp.concatenate([jnp.where(eye, 1.0, 0.0).astype(BF)] * (n // width), axis=0)
    return mul(own, place)


def half_lanes(part):
    return lax.broadcasted_iota(jnp.int32, (ROWS, LANES), 1) // 64 == part


def add_into(ref, at, other):
    ref[at] = (ref[at].astype(F32) + other.astype(F32)).astype(BF)


BIG = (
    ("inputs", "order", "cotangent", "places")
    + ("e_project", "e_out", "e_up", "e_down", "embed", "d_project", "d_out", "d_up", "d_down")
)
SMALL = (
    ("live", "e_gain_a", "e_shift_a", "e_bias_q", "e_bias_v", "e_bias_out", "e_gain_b")
    + ("e_shift_b", "e_bias_up", "e_bias_down", "embed_bias", "mask", "d_gain_a", "d_shift_a")
    + ("d_bias_q", "d_bias_v", "d_bias_out", "d_gain_b", "d_shift_b", "d_bias_up", "d_bias_down")
)
OUTS = ("grad_x", "decoded", "final_hbm", "weightsT_hbm", "keep_active", "keep_middle")
SCRATCH = (
    ("final", "tot_d", "got_c", "got_x", "got_z", "got_zf", "vec", "x_raw", "order_own", "cot_own")
    + ("cot_got", "mixT", "mixT_got", "part_own", "part_got")
    + ("x_rows", "normed", "qkv", "soft", "mixed", "middle", "normed_b", "active", "slope", "seen")
    + ("visible", "v_rows", "qT", "kT", "inverse", "tokens", "grad_mid", "gradT")
    + ("mixed32", "soft_inv", "mix32T", "act_got", "down_own", "down_got", "row_sums")
    + ("load_sem", "ring_sem", "c_sem", "x_sem", "z_sem", "zs_sem", "g_sem", "m_sem", "p_sem", "in_sem", "w_sem")
)


class Refs:
    pass


def step_kernel(length, *refs):
    r = Refs()
    for name, ref in zip(BIG + SMALL + OUTS + SCRATCH, refs, strict=True):
        setattr(r, name, ref)
    dp, side = lax.axis_index("dp"), lax.axis_index("seq")
    core, x, z = lax.rem(dp, 2), lax.rem(dp // 2, 2), dp // 4
    by_core = (dp + 1 - 2 * core, side)
    by_x = (dp + 2 - 4 * x, side)
    by_y = (dp, 1 - side)
    above, below = (dp + 4, side), (dp - 4, side)
    wide = r.x_rows.shape[1]
    inner = r.e_up.shape[1]
    count, width = r.tokens.shape
    half = width // 2
    d_inner = r.d_up.shape[1]
    heads = HEADS_DEC // 2
    size = half // heads
    steps = heads // STEP_HEADS
    scale = size ** (-0.5)
    rows_e, rows_d = wide // 16, width // 16
    own = pl.multiple_of(side * half, half)
    other = pl.multiple_of((1 - side) * half, half)

    def load(src, dst, at):
        return pltpu.make_async_copy(src, dst, r.load_sem.at[at])

    def load_all(pairs, first):
        copies = [load(src, dst, first + at) for at, (src, dst) in enumerate(pairs)]
        for copy in copies:
            copy.start()
        return copies

    def remote(src, dst, sems, at, device):
        return pltpu.make_async_remote_copy(
            src_ref=src,
            dst_ref=dst,
            send_sem=sems.at[(0,) + at],
            recv_sem=sems.at[(1,) + at],
            device_id=device,
            device_id_type=MESH,
        )

    def greet(device):
        pl.semaphore_signal(
            pltpu.get_barrier_semaphore(), inc=1, device_id=device, device_id_type=MESH
        )

    box = Refs()
    box.next = 0

    def z_sends(turn, up):
        return (z < 3) & (turn >= z) if up else (z > 0) & (turn >= 3 - z)

    def z_gets(turn, up):
        return (z > 0) & (turn >= z - 1) if up else (z < 3) & (turn >= 2 - z)

    def got_rows(i):
        return pl.ds(*CHUNKS[i])

    def held(i):
        start, rows = CHUNKS[i]
        if start < D_ROWS:
            return r.tot_d, pl.ds(start, rows)
        return box.tot_e, pl.ds(start - D_ROWS, rows)

    def zf_rows(i):
        before = sum(CHUNKS[j][1] for j in Z_FIRST if j < i)
        return pl.ds(before, CHUNKS[i][1])

    def z_copy(i, turn, up):
        way = 0 if up else 1
        k = jnp.minimum(z + 3 - turn, 3) if up else jnp.maximum(z - 3 + turn, 0)
        ref, at = held(i)
        if i in Z_FIRST:
            src, dst = ref.at[k, :, core, at], r.got_zf.at[way, turn, :, zf_rows(i)]
        else:
            src, dst = ref.at[k, x, core, at], r.got_z.at[way, turn, got_rows(i)]
        return pltpu.make_async_remote_copy(
            src_ref=src,
            dst_ref=dst,
            send_sem=r.zs_sem.at[i, way],
            recv_sem=r.z_sem.at[i, turn, way],
            device_id=above if up else below,
            device_id_type=MESH,
        )

    def z_start(i, turn):
        for up in (True, False):

            @pl.when(z_sends(turn, up))
            def _():
                z_copy(i, turn, up).start()

    def z_finish(i, turn):
        ref, at = held(i)
        for up in (True, False):

            @pl.when(z_gets(turn, up))
            def _():
                z_copy(i, turn, up).wait_recv()
                way = 0 if up else 1
                k = z + 2 - turn if up else z - 2 + turn
                if i in Z_FIRST:
                    add_into(ref, (k, slice(None), core, at), r.got_zf[way, turn, :, zf_rows(i)])
                else:
                    add_into(ref, (k, x, core, at), r.got_z[way, turn, got_rows(i)])

            @pl.when(z_sends(turn, up))
            def _():
                z_copy(i, turn, up).wait_send()

    def c_copy(i):
        ref, at = held(i)
        if i in X_DONE:
            dst = r.got_c.at[:, x, got_rows(i)]
            return remote(ref.at[:, x, 1 - core, at], dst, r.c_sem, (i,), by_core)
        dst = r.got_c.at[:, :, got_rows(i)]
        return remote(ref.at[:, :, 1 - core, at], dst, r.c_sem, (i,), by_core)

    def x_copy(i):
        ref, at = held(i)
        if i in Z_FIRST:
            dst = r.got_x.at[0, got_rows(i)]
            return remote(ref.at[z, 1 - x, core, at], dst, r.x_sem, (i,), by_x)
        dst = r.got_x.at[:, got_rows(i)]
        return remote(ref.at[:, 1 - x, core, at], dst, r.x_sem, (i,), by_x)

    def g_copy(i):
        ref = r.final.at[side, got_rows(i)]
        return remote(ref, ref, r.g_sem, (i,), by_y)

    def g_start(i):
        ref, at = held(i)
        r.final[side, got_rows(i)] = ref[z, x, core, at]
        g_copy(i).start()

    def advance(i, stage):
        ref, at = held(i)
        if stage == "c":
            c_copy(i).wait()
            if i in X_DONE:
                add_into(ref, (slice(None), x, core, at), r.got_c[:, x, got_rows(i)])
            else:
                add_into(ref, (slice(None), slice(None), core, at), r.got_c[:, :, got_rows(i)])
            if i in Z_FIRST + X_DONE:
                z_start(i, 0)
            else:
                x_copy(i).start()
        elif stage == "x":
            x_copy(i).wait()
            if i in Z_FIRST:
                add_into(ref, (z, x, core, at), r.got_x[0, got_rows(i)])
                g_start(i)
            else:
                add_into(ref, (slice(None), x, core, at), r.got_x[:, got_rows(i)])
                z_start(i, 0)
        else:
            turn = int(stage[1])
            z_finish(i, turn)
            if turn < 2:
                z_start(i, turn + 1)
            elif i in Z_FIRST:
                x_copy(i).start()
            else:
                g_start(i)

    def tick(name):
        for i, stage in PLAN.get(name, ()):
            advance(i, stage)

    def ready(rows):
        while box.next < len(CHUNKS) and sum(CHUNKS[box.next]) <= rows:
            if box.next not in X_DONE:
                c_copy(box.next).start()
            box.next += 1

    def store(ref, start, rows, grad):
        for tile in range(grad.shape[1] // LANES):
            part = grad[:, tile * LANES : (tile + 1) * LANES].reshape(4, 2, 2, rows, LANES)
            ref[:, :, :, start + tile * rows : start + (tile + 1) * rows, :] = part.astype(BF)

    def place_vector(at, share):
        for d in range(16):
            r.vec[d // 4, (d // 2) % 2, d % 2, at, :] = share[d, :]

    def half_of(total):
        return pl.ds(pl.multiple_of(side * (total // 2), LANES), total // 2)

    def x_send():
        return remote(r.inputs, r.x_raw, r.in_sem, (0,), by_y)

    def order_send():
        return remote(r.order, r.order_own, r.in_sem, (1,), by_y)

    def cot_send():
        return remote(r.cotangent, r.cot_got, r.in_sem, (2,), by_y)

    def act_send(k):
        cols = inner // 8
        src = r.active.at[:, pl.ds(pl.multiple_of((2 * k + 1 - x) * cols, LANES), cols)]
        return remote(src, r.act_got.at[k], r.w_sem, (k,), by_x)

    def down_send():
        return remote(r.down_own, r.down_got, r.w_sem, (4,), by_x)

    def onehot():
        slots = jnp.broadcast_to(r.order_own[:, : 2 * LANES], (8, 2 * LANES))
        slots = pltpu.roll(slots, 1, 1)[0:1, :ROWS]
        token = lax.broadcasted_iota(jnp.int32, (1, ROWS), 1)
        slots = jnp.where((token >= 1) & (token < length), slots, -1)
        place = lax.broadcasted_iota(jnp.int32, (count, ROWS), 0)
        return jnp.where(place == slots, 1.0, 0.0)

    def encode(w_project, w_out, w_up, w_down, w_embed):
        weights = load_all(
            (
                (r.e_project, w_project),
                (r.e_out, w_out),
                (r.e_up, w_up),
                (r.e_down, w_down),
                (r.embed, w_embed),
            ),
            0,
        )
        for device in (by_core, by_x, by_y):
            greet(device)

        @pl.when(z < 3)
        def _():
            greet(above)

        @pl.when(z > 0)
        def _():
            greet(below)

        neighbours = 3 + jnp.minimum(z, 1) + jnp.minimum(3 - z, 1)
        pl.semaphore_wait(pltpu.get_barrier_semaphore(), neighbours)

        @pl.when(side == 0)
        def _():
            x_send().start()
            order_send().start()
            here = load_all(((r.inputs, r.x_raw), (r.order, r.order_own)), 5)
            for copy in here:
                copy.wait()

        @pl.when(side == 1)
        def _():
            x_send().wait_recv()

        cot_send().start()
        cot = load(r.cotangent, r.cot_own, 7)
        cot.start()
        r.x_rows[...] = jnp.zeros_like(r.x_rows)
        r.x_rows[:length, :] = r.x_raw[0]
        rows = r.x_rows[...].astype(F32)
        unit, _ = standard(rows)
        normed = (unit * row_of(r.e_gain_a) + row_of(r.e_shift_a)).astype(BF)
        r.normed[...] = normed
        weights[0].wait()
        r.qkv[:, :wide] = (mul(normed, w_project[:, :wide]) + row_of(r.e_bias_q)).astype(BF)
        r.qkv[:, wide : 2 * wide] = mul(normed, w_project[:, wide : 2 * wide]).astype(BF)
        values = mul(normed, w_project[:, 2 * wide :]) + row_of(r.e_bias_v)
        r.qkv[:, 2 * wide :] = values.astype(BF)
        valid = lax.broadcasted_iota(jnp.int32, (ROWS, ROWS), 1) < length
        for pair in range(PAIRS):
            at = pair * LANES
            query = r.qkv[:, at : at + LANES]
            keys = r.qkv[:, wide + at : wide + at + LANES]
            values = r.qkv[:, 2 * wide + at : 2 * wide + at + LANES]
            both, invs = [], []
            for part in range(2):
                mine = jnp.where(half_lanes(part), query, jnp.zeros_like(query))
                scores = jnp.where(valid, mul(mine, keys, 1, 1) * 0.125, -1e30)
                raw = jnp.exp(scores - jnp.max(scores, axis=1, keepdims=True)).astype(BF)
                r.soft[2 * pair + part] = raw
                invs.append(1.0 / jnp.sum(raw.astype(F32), axis=1, keepdims=True))
                both.append(mul(raw, values) * invs[part])
            mixed = jnp.where(half_lanes(0), both[0], both[1])
            r.mixed32[:, at : at + LANES] = mixed
            r.mixed[:, at : at + LANES] = mixed.astype(BF)
            r.soft_inv[:, at : at + LANES] = jnp.where(half_lanes(0), invs[0], invs[1])
        weights[1].wait()
        middle = rows + (mul(r.mixed[...], w_out[...]) + row_of(r.e_bias_out))
        r.middle[...] = middle
        unit, _ = standard(middle)
        normed_b = (unit * row_of(r.e_gain_b) + row_of(r.e_shift_b)).astype(BF)
        r.normed_b[...] = normed_b
        weights[2].wait()
        for part in range(4):
            cols = slice(part * wide, (part + 1) * wide)
            up = mul(normed_b, w_up[:, cols]) + r.e_bias_up[cols][None, :]
            active, slope = gelu_pair(up)
            r.active[:, cols] = active.astype(BF)
            r.slope[:, cols] = slope.astype(BF)
        weights[3].wait()
        for k in range(4):
            act_send(k).start()
        encoded = middle + (mul(r.active[...], w_down[...]) + row_of(r.e_bias_down))
        seen = encoded.astype(BF)
        r.seen[...] = seen
        weights[4].wait()
        r.visible[...] = mul(seen, w_embed[...]) + row_of(r.embed_bias)
        cot.wait()

        @pl.when(side == 0)
        def _():
            x_send().wait_send()
            order_send().wait_send()

        @pl.when(side == 1)
        def _():
            order_send().wait_recv()

    pl.run_scoped(
        encode,
        *[pltpu.VMEM(ref.shape, BF) for ref in (r.e_project, r.e_out, r.e_up, r.e_down, r.embed)],
    )

    def ring_copy(step, ring, out):
        slot = lax.rem(step, 2)
        there = r.weightsT_hbm.at[pl.ds(STEP_HEADS * step, STEP_HEADS)]
        src, dst = (ring.at[slot], there) if out else (there, ring.at[slot])
        return pltpu.make_async_copy(src, dst, r.ring_sem.at[slot])

    def mixed_copy(step):
        rows = pl.ds(pl.multiple_of(step * STEP_HEADS * size, STEP_HEADS * size), STEP_HEADS * size)
        return remote(r.mixT.at[rows], r.mixT_got.at[rows], r.m_sem, (step,), by_y)

    def decode(ring, w_project, places, k_scr, vT_scr):
        loads = load_all(((r.places, places), (r.d_project, w_project)), 0)
        spots = onehot()
        covered = jnp.sum(spots, axis=1, keepdims=True)
        spots = spots.astype(BF)
        visible = r.visible[...]
        high = visible.astype(BF)
        low = (visible - high.astype(F32)).astype(BF)
        placed = mul(spots, high) + mul(spots, low)
        loads[0].wait()
        tokens = (placed + (1.0 - covered) * row_of(r.mask) + places[...]).astype(BF)
        r.tokens[...] = tokens
        unit, _ = standard(tokens.astype(F32))
        normed = (unit * row_of(r.d_gain_a) + row_of(r.d_shift_a)).astype(BF)
        bias_q = r.d_bias_q[pl.ds(own, half)][None, :]
        bias_v = r.d_bias_v[pl.ds(own, half)][None, :]
        loads[1].wait()
        query = (mul(normed, w_project[:, pl.ds(own, half)]) + bias_q).astype(BF)
        keys = mul(normed, w_project[:, pl.ds(pl.multiple_of(width + own, half), half)]).astype(BF)
        at = pl.ds(pl.multiple_of(2 * width + own, half), half)
        values = (mul(normed, w_project[:, at]) + bias_v).astype(BF)
        r.qT[...] = query.T
        r.kT[...] = keys.T
        vT_scr[...] = values.T
        k_scr[...] = keys
        r.v_rows[...] = values
        lane = lax.broadcasted_iota(jnp.int32, (count, half), 1) // size
        ones = jnp.ones((16, count), BF)

        def body(step, carry):
            slot = lax.rem(step, 2)

            @pl.when(step >= 2)
            def _():
                ring_copy(step - 2, ring, True).wait()

            for at in range(STEP_HEADS):
                head = step * STEP_HEADS + at
                rows = pl.ds(pl.multiple_of(head * size, size), size)
                mine = jnp.where(lane == head, k_scr[...], jnp.zeros((), BF))
                scores = mul(mine, r.qT[...])
                top = jnp.max(scores, axis=0, keepdims=True)
                raw = jnp.exp2((scores - top) * (scale * 1.4426950408889634)).astype(BF)
                ring[slot, at] = raw
                mixed = mul(jnp.concatenate([vT_scr[rows, :], ones], axis=0), raw)
                inverse = 1.0 / mixed[size : size + 1]
                r.inverse[head] = inverse
                mixed = mixed[:size] * inverse
                r.mix32T[rows, :] = mixed
                r.mixT[rows, :] = mixed.astype(BF)

            @pl.when(step < steps - 2)
            def _():
                ring_copy(step, ring, True).start()

            mixed_copy(step).start()
            return carry

        lax.fori_loop(0, steps, body, 0)

    def feed(w_out, w_up, w_down, cot, active_scr, inner_scr, middle_scr, out_scr):
        loads = load_all(((r.d_down, w_down), (r.d_out, w_out), (r.d_up, w_up)), 0)
        live = jnp.minimum(r.live[0], 1).astype(F32)
        cot_send().wait()
        mine = r.cot_own[0].astype(F32) * live
        theirs = r.cot_got[0].astype(F32) * live
        first = side == 0
        cot[...] = jnp.concatenate(
            [jnp.where(first, mine, theirs), jnp.where(first, theirs, mine)], axis=0
        ).astype(BF)
        grad = cot[...]
        block = d_inner // 4
        loads[0].wait()
        for part in range(4):
            cols = slice(part * block, (part + 1) * block)
            inner_scr[:, cols] = mul(grad, w_down[cols, :], 1, 1).astype(BF)
        loads[1].wait()
        branch = mul(r.mixT[...], w_out[pl.ds(own, half), :], 0, 0)
        for step in range(steps):
            mixed_copy(step).wait()
        branch = branch + mul(r.mixT_got[...], w_out[pl.ds(other, half), :], 0, 0)
        middle = r.tokens[...].astype(F32) + (branch + row_of(r.d_bias_out))
        middle_scr[...] = middle
        unit, _ = standard(middle)
        normed = (unit * row_of(r.d_gain_b) + row_of(r.d_shift_b)).astype(BF)
        grad = cot[...]
        grad_normed = jnp.zeros((count, width), F32)
        loads[2].wait()
        for part in range(4):
            cols = slice(part * block, (part + 1) * block)
            up = mul(normed, w_up[:, cols]) + r.d_bias_up[cols][None, :]
            active, slope = gelu_pair(up)
            active_scr[:, cols] = active.astype(BF)
            grad_inner = (inner_scr[:, cols].astype(F32) * slope).astype(BF)
            inner_scr[:, cols] = grad_inner
            grad_normed = grad_normed + mul(grad_inner, w_up[:, cols], 1, 1)
            r.row_sums[4 + part : 5 + part, :] = 0.5 * sums(grad_inner.astype(F32))
        top = pl.multiple_of(side * 384, 128)
        keep = (
            load(active_scr.at[pl.ds(top, 400)], r.keep_active, 3),
            load(middle_scr.at[pl.ds(top, 400)], r.keep_middle, 4),
        )
        for copy in keep:
            copy.start()
        store(r.tot_d, D_DOWN, d_inner // 16, mul(active_scr[...], cot[:, half_of(width)], 0, 0))
        ready(D_UP)
        for piece in range(2):
            span = d_inner // 4
            at = pl.multiple_of(side * 2 * span + piece * span, span)
            grad_w = mul(normed, inner_scr[:, pl.ds(at, span)], 0, 0)
            store(r.tot_d, D_UP + piece * (span // LANES) * rows_d, rows_d, grad_w)
        unit, spread = standard(middle_scr[...])
        grad_middle = grad.astype(F32) + standard_back(unit, spread, grad_normed * row_of(r.d_gain_b))
        r.grad_mid[...] = grad_middle
        grad_out = grad_middle.astype(BF)
        out_scr[...] = grad_out
        r.gradT[...] = mul(w_out[pl.ds(own, half), :], grad_out, 1, 1).astype(BF)
        for at, row in enumerate(
            (
                sums(grad_out.astype(F32)),
                sums(grad_normed * unit),
                sums(grad_normed),
                sums(grad.astype(F32)),
            )
        ):
            r.row_sums[at : at + 1, :] = 0.5 * row
        cols = out_scr[:, half_of(width)]
        low, high = mul(r.mixT[...], cols), mul(r.mixT_got[...], cols)
        zs = half // rows_d // 4
        for which, part in ((side, low), (1 - side, high)):
            for tile in range(half // LANES):
                block_of = part[:, tile * LANES : (tile + 1) * LANES]
                block_of = block_of.reshape(zs, 2, 2, rows_d, LANES).astype(BF)
                at = D_OUT + tile * rows_d
                r.tot_d[pl.ds(which * zs, zs), :, :, at : at + rows_d, :] = block_of
        ready(D_PROJECT)
        for copy in keep:
            copy.wait()

    def part_copy():
        return remote(r.part_own, r.part_got, r.p_sem, (), by_y)

    def attend_back(ring, dq, dk, dv, w_project, w_down, kept_active, kept_middle):
        kept = load_all(
            ((r.d_down, w_down), (r.keep_active, kept_active), (r.keep_middle, kept_middle)), 0
        )
        project = load(r.d_project, w_project, 3)
        project.start()
        lane = lax.broadcasted_iota(jnp.int32, (count, half), 1) // size
        tick("heads")

        def body(now, carry):
            step = steps - 1 - now
            slot = lax.rem(step, 2)

            @pl.when(now >= 2)
            def _():
                ring_copy(step, ring, False).wait()

            for at in range(STEP_HEADS):
                head = step * STEP_HEADS + at
                rows = pl.ds(pl.multiple_of(head * size, size), size)
                values = jnp.where(lane == head, r.v_rows[...], jnp.zeros((), BF))
                inv = r.inverse[head]
                grad = (r.gradT[rows, :].astype(F32) * inv).astype(BF)
                delta = jnp.sum(grad.astype(F32) * r.mix32T[rows, :], axis=0, keepdims=True)
                every = (r.gradT[...].astype(F32) * inv).astype(BF)
                raw = ring[slot, at]
                grad_scores = raw.astype(F32) * ((mul(values, every) - delta) * scale)
                grad_scores = grad_scores.astype(BF)
                dv[rows, :] = mul(grad, raw, 1, 1).astype(BF)
                dk[rows, :] = mul(r.qT[rows, :], grad_scores, 1, 1).astype(BF)
                dq[rows, :] = mul(r.kT[rows, :], grad_scores).astype(BF)

            @pl.when(step >= 2)
            def _():
                ring_copy(step - 2, ring, False).start()

            for done in range(steps - 1):
                if f"heads{done}" in PLAN:

                    @pl.when(now == done)
                    def _():
                        tick(f"heads{done}")

            return carry

        lax.fori_loop(0, steps, body, 0)
        tick("after_heads")
        project.wait()
        unit, spread = standard(r.tokens[...].astype(F32))
        grad_normed = jnp.zeros((count, width), F32)
        for at, piece in enumerate((dq, dk, dv)):
            cols = pl.ds(pl.multiple_of(at * width + own, half), half)
            grad_normed = grad_normed + mul(piece[...], w_project[:, cols], 0, 1)
        grad = standard_back(unit, spread, grad_normed * row_of(r.d_gain_a))
        grad = grad + 0.5 * r.grad_mid[...]
        high = grad.astype(BF)
        low = (grad - high.astype(F32)).astype(BF)
        spots = onehot().astype(BF)
        gathered = mul(spots, high, 0, 0) + mul(spots, low, 0, 0)
        r.part_own[...] = gathered.astype(BF)
        part_copy().start()
        tick("gathered")
        normed = (unit * row_of(r.d_gain_a) + row_of(r.d_shift_a)).astype(BF)
        for at, piece in enumerate((dq, dk, dv)):
            start = D_PROJECT + at * (half // LANES) * rows_d
            store(r.tot_d, start, rows_d, mul(normed, piece[...], 0, 1))
        ready(D_ROWS)
        shares = [
            shares_of(row, width)
            for row in (
                sums(grad_normed * unit),
                sums(grad_normed),
                sums(grad) - sums(gathered),
            )
        ]
        for piece in (dq, dv):
            column = jnp.sum(piece[...].astype(F32), axis=1, keepdims=True)
            square = lax.broadcasted_iota(jnp.int32, (half, half), 0) == lax.broadcasted_iota(
                jnp.int32, (half, half), 1
            )
            shares.append(shares_of(sums(jnp.where(square, column, 0.0)), width, own))
        for at, share in enumerate(shares):
            place_vector(5 + at, share)
        for at in range(4):
            place_vector(at, shares_of(r.row_sums[at : at + 1, :], width))
        total = jnp.zeros((16, LANES), F32)
        for part in range(4):
            row = r.row_sums[4 + part : 5 + part, :]
            total = total + shares_of(row, d_inner, part * (d_inner // 4))
        place_vector(4, total)
        for copy in kept:
            copy.wait()
        live = jnp.minimum(r.live[0], 1).astype(F32)
        decoded = mul(kept_active[...], w_down[...]) + row_of(r.d_bias_down)
        kept_middle[...] = (kept_middle[...] + decoded) * live
        block = r.decoded.shape[0]
        r.decoded[...] = kept_middle[pl.ds(pl.multiple_of(side * 8, 8), block), :].astype(BF)

    def encode_back(w_up, w_down, w_embed, w_project, w_out, tot_e, inner_scr, *rest):
        wide_scr, down_scr, out_scr = rest
        box.tot_e = tot_e
        loads = load_all(
            (
                (r.embed, w_embed),
                (r.e_down, w_down),
                (r.e_up, w_up),
                (r.e_out, w_out),
                (r.e_project, w_project),
            ),
            0,
        )

        def vector(at, row):
            place_vector(10 + at, shares_of(0.5 * row, row.shape[1]))

        def put(start, rows, grad):
            store(tot_e, start - D_ROWS, rows, grad)

        tick("open")
        loads[0].wait()
        part_copy().wait()
        gathered = r.part_own[...].astype(F32) + r.part_got[...].astype(F32)
        grad_visible = gathered.astype(BF)
        r.part_own[...] = grad_visible
        grad_encoded = mul(grad_visible, w_embed[...], 1, 1)
        grad_down = grad_encoded.astype(BF)
        down_scr[...] = grad_down
        r.down_own[...] = down_scr[:, half_of(wide)]
        down_send().start()
        put(E_EMBED, rows_e, mul(r.seen[...], r.part_own[:, half_of(width)], 0, 0))
        ready(E_DOWN)
        tick("embed")
        grad_normed = jnp.zeros((ROWS, wide), F32)
        loads[1].wait()
        loads[2].wait()
        for part in range(4):
            cols = slice(part * wide, (part + 1) * wide)
            grad_inner = mul(grad_down, w_down[cols, :], 1, 1) * r.slope[:, cols].astype(F32)
            grad_inner = grad_inner.astype(BF)
            inner_scr[:, cols] = grad_inner
            grad_normed = grad_normed + mul(grad_inner, w_up[:, cols], 1, 1)
            tick(f"part{part}")
        span = inner // 6
        for piece in range(3):
            at = pl.multiple_of(side * (inner // 2) + piece * span, LANES)
            grad_w = mul(r.normed_b[...], inner_scr[:, pl.ds(at, span)], 0, 0)
            put(E_UP + piece * (span // LANES) * rows_e, rows_e, grad_w)
            ready(E_UP + (piece + 1) * (span // LANES) * rows_e)
            tick(f"up{piece}")
        for k in range(4):
            act_send(k).wait()
        down_send().wait()
        cols = inner // 8
        for k in range(4):
            here = pl.ds(pl.multiple_of((2 * k + x) * cols, LANES), cols)
            grad_w = mul(r.active[:, here], r.down_own[...], 0, 0)
            grad_w = (grad_w + mul(r.act_got[k], r.down_got[...], 0, 0)).astype(BF)
            for tile in range(wide // 2 // LANES):
                part = grad_w[:, tile * LANES : (tile + 1) * LANES].reshape(2, cols // 2, LANES)
                at = E_DOWN - D_ROWS + tile * (cols // 2)
                tot_e[k, x, :, at : at + cols // 2, :] = part
        for i in X_DONE:
            c_copy(i).start()
        tick("down")
        unit, spread = standard(r.middle[...])
        grad_middle = grad_encoded + standard_back(unit, spread, grad_normed * row_of(r.e_gain_b))
        grad_out = grad_middle.astype(BF)
        out_scr[...] = grad_out
        tick("norm")
        loads[3].wait()
        loads[4].wait()
        put(E_OUT, rows_e, mul(r.mixed[...], out_scr[:, half_of(wide)], 0, 0))
        ready(E_PROJECT)
        tick("out")
        vector(2, sums(grad_out.astype(F32)))
        vector(3, sums(grad_normed * unit))
        vector(4, sums(grad_normed))
        vector(5, sums(grad_down.astype(F32)))
        vector(6, sums(grad_visible.astype(F32)))
        shares = jnp.zeros((16, 2 * LANES), F32)
        for part in range(4):
            cols = slice(part * wide, (part + 1) * wide)
            row = 0.5 * sums(inner_scr[:, cols].astype(F32))
            shares = shares + shares_of(row, inner, part * wide)
        place_vector(19, shares[:, :LANES])
        place_vector(20, shares[:, LANES:])
        tick("sums")
        grad_mixed = mul(grad_out, w_out[...], 1, 1)
        for pair in range(PAIRS):
            at = pair * LANES
            query = r.qkv[:, at : at + LANES]
            keys = r.qkv[:, wide + at : wide + at + LANES]
            values = r.qkv[:, 2 * wide + at : 2 * wide + at + LANES]
            grad_pair = grad_mixed[:, at : at + LANES]
            grad_low = (grad_pair * r.soft_inv[:, at : at + LANES]).astype(BF)
            dot_pair = grad_low.astype(F32) * r.mixed32[:, at : at + LANES]
            found = []
            for part in range(2):
                lanes = half_lanes(part)
                delta = jnp.sum(jnp.where(lanes, dot_pair, 0.0), axis=1, keepdims=True)
                mine = jnp.where(lanes, grad_low, jnp.zeros_like(grad_low))
                soft = r.soft[2 * pair + part]
                grad_scores = soft.astype(F32) * ((mul(mine, values, 1, 1) - delta) * 0.125)
                grad_scores = grad_scores.astype(BF)
                found.append(
                    (
                        mul(grad_scores, keys),
                        mul(grad_scores, query, 0, 0),
                        mul(soft, grad_low, 0, 0),
                    )
                )
            for kind in range(3):
                both = jnp.where(half_lanes(0), found[0][kind], found[1][kind])
                wide_scr[:, kind * wide + at : kind * wide + at + LANES] = both.astype(BF)
            tick(f"pair{pair}")
        put(E_PROJECT, rows_e, mul(r.normed[...], wide_scr[:, half_of(3 * wide)], 0, 0))
        ready(E_VECTOR)
        tick("project")
        vector(7, sums(wide_scr[:, :wide].astype(F32)))
        vector(8, sums(wide_scr[:, 2 * wide :].astype(F32)))
        grad_normed = mul(wide_scr[...], w_project[...], 1, 1)
        unit, spread = standard(r.x_rows[...].astype(F32))
        vector(0, sums(grad_normed * unit))
        vector(1, sums(grad_normed))
        r.vec[:, :, :, 21:, :] = jnp.zeros((4, 2, 2, V_ROWS - 21, LANES), F32)
        tot_e[:, :, :, E_VECTOR - D_ROWS :, :] = r.vec[...].astype(BF)
        ready(T_ROWS)
        tick("vectors")
        grad_x = grad_middle + standard_back(unit, spread, grad_normed * row_of(r.e_gain_a))
        r.mixed32[...] = jnp.where(side == 0, grad_x, 0.0)
        result = load(r.mixed32, r.grad_x, 0)
        result.start()
        tick("after")
        finals = []
        for i in range(len(CHUNKS)):
            g_copy(i).wait()
            at = got_rows(i)
            finals.append(load(r.final.at[:, at], r.final_hbm.at[:, at], 1 + i))
            finals[i].start()
        for copy in [result] + finals:
            copy.wait()

    def decoder(ring):
        pl.run_scoped(
            partial(decode, ring),
            pltpu.VMEM(r.d_project.shape, BF),
            pltpu.VMEM(r.places.shape, F32),
            pltpu.VMEM((count, half), BF),
            pltpu.VMEM((half, count), BF),
        )
        pl.run_scoped(
            feed,
            pltpu.VMEM(r.d_out.shape, BF),
            pltpu.VMEM(r.d_up.shape, BF),
            pltpu.VMEM(r.d_down.shape, BF),
            pltpu.VMEM((count, width), BF),
            pltpu.VMEM((count, d_inner), BF),
            pltpu.VMEM((count, d_inner), BF),
            pltpu.VMEM((count, width), F32),
            pltpu.VMEM((count, width), BF),
        )
        pl.run_scoped(
            partial(attend_back, ring),
            pltpu.VMEM((half, count), BF),
            pltpu.VMEM((half, count), BF),
            pltpu.VMEM((half, count), BF),
            pltpu.VMEM(r.d_project.shape, BF),
            pltpu.VMEM(r.d_down.shape, BF),
            pltpu.VMEM(r.keep_active.shape, BF),
            pltpu.VMEM(r.keep_middle.shape, F32),
        )

    pl.run_scoped(decoder, pltpu.VMEM((2, STEP_HEADS, count, count), BF))
    pl.run_scoped(
        encode_back,
        *[
            pltpu.VMEM(ref.shape, BF)
            for ref in (r.e_up, r.e_down, r.embed, r.e_project, r.e_out)
        ],
        pltpu.VMEM((4, 2, 2, T_ROWS - D_ROWS, LANES), BF),
        pltpu.VMEM((ROWS, inner), BF),
        pltpu.VMEM((ROWS, 3 * wide), BF),
        pltpu.VMEM((ROWS, wide), BF),
        pltpu.VMEM((ROWS, wide), BF),
    )


def unpack_kernel(final_hbm, grad_x_hbm, decoded_hbm, *refs):
    decoded, input_grad, *outs, final, grad_x, decoded_in, sem = refs
    pairs = ((grad_x_hbm, grad_x), (decoded_hbm, decoded_in), (final_hbm, final))
    copies = [pltpu.make_async_copy(*pair, sem.at[at]) for at, pair in enumerate(pairs)]
    for copy in copies:
        copy.start()
    copies[0].wait()
    length = input_grad.shape[0]
    input_grad[...] = grad_x[:length, :].reshape(length, 1, grad_x.shape[1])
    copies[1].wait()
    decoded[0] = decoded_in[...]
    copies[2].wait()
    (
        enc_gain_a,
        enc_shift_a,
        enc_project,
        enc_bias_q,
        enc_bias_v,
        enc_out,
        enc_bias_out,
        enc_gain_b,
        enc_shift_b,
        enc_up,
        enc_bias_up,
        enc_down,
        enc_bias_down,
        embed_w,
        embed_b,
        mask,
        dec_gain_a,
        dec_shift_a,
        dec_project,
        dec_bias_q,
        dec_bias_v,
        dec_out,
        dec_bias_out,
        dec_gain_b,
        dec_shift_b,
        dec_up,
        dec_bias_up,
        dec_down,
        dec_bias_down,
    ) = outs
    for ref, start in (
        (enc_project, E_PROJECT),
        (enc_out, E_OUT),
        (enc_up, E_UP),
        (enc_down, E_DOWN),
        (embed_w, E_EMBED),
        (dec_out, D_OUT),
        (dec_up, D_UP),
        (dec_down, D_DOWN),
    ):
        rows, cols = ref.shape
        half = cols // 2
        for side in range(2):
            for tile in range(half // LANES):
                at = start + tile * rows
                to = side * half + tile * LANES
                ref[:, to : to + LANES] = final[side, at : at + rows, :].astype(F32)
    rows, cols = dec_project.shape
    for side in range(2):
        for tile in range(cols // 2 // LANES):
            at = D_PROJECT + tile * rows
            each = cols // 6 // LANES
            to = (tile // each) * (cols // 3) + side * (cols // 6) + (tile % each) * LANES
            dec_project[:, to : to + LANES] = final[side, at : at + rows, :].astype(F32)
    vector = final[0, E_VECTOR:, :].astype(F32) + final[1, E_VECTOR:, :].astype(F32)
    places = (
        (dec_bias_out, dec_gain_b, dec_shift_b, dec_bias_down, dec_bias_up)
        + (dec_gain_a, dec_shift_a, mask, dec_bias_q, dec_bias_v)
        + (enc_gain_a, enc_shift_a, enc_bias_out, enc_gain_b, enc_shift_b)
        + (enc_bias_down, embed_b, enc_bias_q, enc_bias_v)
    )
    for at, ref in enumerate(places):
        ref[...] = vector[at, : ref.shape[0]]
    at = len(places)
    rest = enc_bias_up.shape[0] - LANES
    enc_bias_up[:LANES] = vector[at]
    enc_bias_up[LANES:] = vector[at + 1, :rest]


def place_table(width):
    quarter = width // 4
    omega = 1.0 / 10000.0 ** (np.arange(quarter).astype(np.float32) / np.float32(quarter))
    at = np.arange(PATCHES)
    first = (at // GRID).astype(np.float32)[:, None] * omega[None, :].astype(np.float32)
    second = (at % GRID).astype(np.float32)[:, None] * omega[None, :].astype(np.float32)
    parts = [np.sin(first), np.cos(first), np.sin(second), np.cos(second)]
    return jnp.asarray(np.concatenate(parts, axis=1).astype(np.float32))


def paired_step(
    inputs,
    patch_order,
    image_count,
    cotangent,
    enc_gain_attn,
    enc_shift_attn,
    enc_project,
    enc_bias_query,
    enc_bias_value,
    enc_out,
    enc_bias_out,
    enc_gain_mlp,
    enc_shift_mlp,
    enc_up,
    enc_bias_up,
    enc_down,
    enc_bias_down,
    embed_weight,
    embed_bias,
    mask_token,
    dec_gain_attn,
    dec_shift_attn,
    dec_project,
    dec_bias_query,
    dec_bias_value,
    dec_out,
    dec_bias_out,
    dec_gain_mlp,
    dec_shift_mlp,
    dec_up,
    dec_bias_up,
    dec_down,
    dec_bias_down,
):
    data_size = lax.axis_size("dp")
    length, width = inputs.shape[1:]
    block, dec_width = cotangent.shape[1:]
    count = 2 * block
    half = dec_width // 2
    inner = enc_up.shape[1]
    heads = HEADS_DEC // 2
    chunks = len(CHUNKS)
    big = (
        (inputs, patch_order, cotangent, place_table(dec_width))
        + (enc_project, enc_out, enc_up, enc_down, embed_weight)
        + (dec_project, dec_out, dec_up, dec_down)
    )
    small = (
        (image_count, enc_gain_attn, enc_shift_attn, enc_bias_query, enc_bias_value)
        + (enc_bias_out, enc_gain_mlp, enc_shift_mlp, enc_bias_up, enc_bias_down, embed_bias)
        + (mask_token, dec_gain_attn, dec_shift_attn, dec_bias_query, dec_bias_value)
        + (dec_bias_out, dec_gain_mlp, dec_shift_mlp, dec_bias_up, dec_bias_down)
    )
    vmem, dma = pltpu.VMEM, pltpu.SemaphoreType.DMA
    grad_x, decoded, final, *_ = pl.pallas_call(
        partial(step_kernel, length),
        in_specs=[ANYWHERE] * len(big)
        + [pl.BlockSpec(memory_space=pltpu.SMEM)]
        + [WHOLE] * (len(small) - 1),
        out_specs=[ANYWHERE, WHOLE] + [ANYWHERE] * 4,
        out_shape=[
            jax.ShapeDtypeStruct((ROWS, width), F32),
            jax.ShapeDtypeStruct((block, dec_width), BF),
            jax.ShapeDtypeStruct((2, T_ROWS, LANES), BF),
            jax.ShapeDtypeStruct((heads - 2 * STEP_HEADS, count, count), BF),
            jax.ShapeDtypeStruct((400, dec_up.shape[1]), BF),
            jax.ShapeDtypeStruct((400, dec_width), F32),
        ],
        scratch_shapes=[
            vmem((2, T_ROWS, LANES), BF),
            vmem((4, 2, 2, D_ROWS, LANES), BF),
            vmem((4, 2, T_ROWS, LANES), BF),
            vmem((4, T_ROWS, LANES), BF),
            vmem((2, 3, T_ROWS, LANES), BF),
            vmem((2, 3, 2, max(16, sum(CHUNKS[i][1] for i in Z_FIRST)), LANES), BF),
            vmem((4, 2, 2, V_ROWS, LANES), F32),
            vmem(inputs.shape, BF),
            vmem(patch_order.shape, jnp.int32),
            vmem(cotangent.shape, BF),
            vmem(cotangent.shape, BF),
            vmem((half, count), BF),
            vmem((half, count), BF),
            vmem((ROWS, dec_width), BF),
            vmem((ROWS, dec_width), BF),
            vmem((ROWS, width), BF),
            vmem((ROWS, width), BF),
            vmem((ROWS, 3 * width), BF),
            vmem((HEADS_ENC, ROWS, ROWS), BF),
            vmem((ROWS, width), BF),
            vmem((ROWS, width), F32),
            vmem((ROWS, width), BF),
            vmem((ROWS, inner), BF),
            vmem((ROWS, inner), BF),
            vmem((ROWS, width), BF),
            vmem((ROWS, dec_width), F32),
            vmem((count, half), BF),
            vmem((half, count), BF),
            vmem((half, count), BF),
            vmem((heads, 1, count), F32),
            vmem((count, dec_width), BF),
            vmem((count, dec_width), F32),
            vmem((half, count), BF),
            vmem((ROWS, width), F32),
            vmem((ROWS, width), F32),
            vmem((half, count), F32),
            vmem((4, ROWS, inner // 8), BF),
            vmem((ROWS, width // 2), BF),
            vmem((ROWS, width // 2), BF),
            vmem((8, dec_width), F32),
            dma((1 + max(chunks, 7),)),
            dma((2,)),
            dma((2, chunks)),
            dma((2, chunks)),
            dma((chunks, 3, 2)),
            dma((chunks, 2)),
            dma((2, chunks)),
            dma((2, heads // STEP_HEADS)),
            dma((2,)),
            dma((2, 3)),
            dma((2, 5)),
        ],
        compiler_params=pltpu.CompilerParams(
            vmem_limit_bytes=VMEM_CAP, collective_id=1, has_side_effects=True
        ),
        cost_estimate=pl.CostEstimate(
            flops=50_000_000_000, bytes_accessed=60_000_000, transcendentals=0
        ),
        name="step",
    )(*big, *small)

    def share(array):
        return jax.ShapeDtypeStruct((array.shape[0] // data_size,) + array.shape[1:], F32)

    weights_in = (
        (enc_gain_attn, enc_shift_attn, enc_project, enc_bias_query, enc_bias_value, enc_out)
        + (enc_bias_out, enc_gain_mlp, enc_shift_mlp, enc_up, enc_bias_up, enc_down)
        + (enc_bias_down, embed_weight, embed_bias, mask_token, dec_gain_attn, dec_shift_attn)
        + (dec_project, dec_bias_query, dec_bias_value, dec_out, dec_bias_out, dec_gain_mlp)
        + (dec_shift_mlp, dec_up, dec_bias_up, dec_down, dec_bias_down)
    )
    outs = [
        jax.ShapeDtypeStruct(cotangent.shape, BF),
        jax.ShapeDtypeStruct((length, 1, width), F32),
    ] + [share(array) for array in weights_in]
    results = pl.pallas_call(
        unpack_kernel,
        out_shape=outs,
        in_specs=[ANYWHERE] * 3,
        out_specs=[WHOLE] * len(outs),
        scratch_shapes=[
            vmem(final.shape, BF),
            vmem(grad_x.shape, F32),
            vmem(decoded.shape, BF),
            dma((3,)),
        ],
        compiler_params=pltpu.CompilerParams(vmem_limit_bytes=VMEM_CAP),
        name="unpack",
    )(final, grad_x, decoded)
    return (results[0], results[1].transpose(1, 0, 2)) + tuple(results[2:])


def solution(mesh):
    in_specs = (
        P(("dp", "seq"), None, None),
        P(("dp", "seq"), None),
        P("dp"),
        P("dp", "seq", None),
        P(),
        P(),
        P(),
        P(),
        P(),
        P(),
        P(),
        P(),
        P(),
        P(),
        P(),
        P(),
        P(),
        P(),
        P(),
        P(),
        P(),
        P(),
        P(),
        P(),
        P(),
        P(),
        P(),
        P(),
        P(),
        P(),
        P(),
        P(),
        P(),
    )
    out_specs = (
        P("dp", "seq", None),
        P(("dp", "seq"), None, None),
        P("dp"),
        P("dp"),
        P("dp", None),
        P("dp"),
        P("dp"),
        P("dp", None),
        P("dp"),
        P("dp"),
        P("dp"),
        P("dp", None),
        P("dp"),
        P("dp", None),
        P("dp"),
        P("dp", None),
        P("dp"),
        P("dp"),
        P("dp"),
        P("dp"),
        P("dp", None),
        P("dp"),
        P("dp"),
        P("dp", None),
        P("dp"),
        P("dp"),
        P("dp"),
        P("dp", None),
        P("dp"),
        P("dp", None),
        P("dp"),
    )
    paired = dict(mesh.shape) == {"dp": 16, "seq": 2}
    return jax.shard_map(
        paired_step if paired else per_device, mesh=mesh, in_specs=in_specs, out_specs=out_specs, check_vma=False
    )
```
